256 devices in a mesh: video: 2 (over x_lo), frame: 16 (over z, x_hi), head: 8 (over y, core).
Axes of the slice: x: 4 (x_hi: 2, x_lo: 2; x = x_hi * 2 + x_lo), y: 4, z: 8, core: 2. Of those that a mesh axis runs over, the one named last changes fastest.
Arguments:
- query: bfloat16 [49152, 3072], P(('video', 'frame'), 'head'), parts along dimension 0, may hold values from -100 to 100
- keys: bfloat16 [49152, 3072], P(('video', 'frame'), 'head'), parts along dimension 0, may hold values from -4.04 to 4.04
- values: bfloat16 [49152, 3072], P(('video', 'frame'), 'head'), parts along dimension 0, may hold values from -6 to 6
- out_weight: bfloat16 [3072, 3072], P('head'), may hold values from -0.5 to 0.5
- tile_lists: int32 [128, 12], P(('video', 'frame')), parts along dimension 0, may hold values from 0 to 63, as said below
Outputs:
- mixed: bfloat16 [49152, 3072], P(('video', 'frame', 'head')), parts along dimension 0
The draws below stay inside these ranges and needn't reach their ends.
There are 2 independent parts, one for each index of `video`. The reference program is written for one: setup_inputs(seed, part) draws one part's arguments, and reference() takes and returns one part's arrays. A program takes and returns all parts, laid end to end along the dimension named above; an argument that names none is the same for every part. Nothing has to cross between parts.
Inputs may be any that keep to these rules, and one draw needn't show every extreme that they name: `tile_lists`: row t names 12 different tiles; the first is tile t itself, the second lies exactly 2 slabs from tile t's slab, and all lie at most 2 slabs from it (the slab of tile u is u // 4).
All inputs are finite; a program needn't handle non-finite values.
Results may differ from the reference program's by a relative error of at most 0.017.
Values may be sent and summed in bfloat16 or wider, within the bound.
No kernel may reach another device: no remote copies, remote signals or barrier semaphores. Data moves between devices by JAX's collectives and lax.ppermute only.
A program may use at most 192 MiB of HBM per device.

```python
import math
import jax
import jax.numpy as jnp
from jax import lax

D = 3072
HEADS = 24
HD = 128
TPS = 4
TILE = 384
REACH = 2
KT = 12
NTILES = 64
TOKENS = 24576
HEAD_COLS = 384


def shared_base(key):
    return jnp.clip(jax.random.normal(key, (TOKENS, HEADS * HD), jnp.float32), -4.0, 4.0)


def draw_keys(key, part):
    base = shared_base(key)
    return base.astype(jnp.bfloat16)


def draw_query(key, part):
    key = jax.random.fold_in(key, 7)
    first_key = jax.random.fold_in(key, 0)
    result = 2.0 * jnp.clip(jax.random.normal(first_key, (TOKENS, HEADS * HD), jnp.float32), -4.0, 4.0)
    return result.astype(jnp.bfloat16)


def draw_tile_lists(key, part):
    key = jax.random.fold_in(key, 5)
    spot_key, noise_key = jax.random.split(key)
    slab_count = NTILES // TPS
    tile_ids = jnp.arange(NTILES, dtype=jnp.int32)
    tile_slab = tile_ids // TPS
    candidate = jnp.arange((2 * REACH + 1) * TPS, dtype=jnp.int32)
    target = tile_slab[:, None] + candidate[None, :] // TPS - REACH
    usable = (target >= 0) & (target < slab_count)
    far_offset = jnp.where(tile_slab + REACH < slab_count, REACH, -REACH)
    far_spot = jax.random.randint(spot_key, (NTILES,), 0, TPS, dtype=jnp.int32)
    far_cand = (far_offset + REACH) * TPS + far_spot
    own_cand = REACH * TPS + tile_ids % TPS
    noise = jax.random.randint(noise_key, (NTILES, (2 * REACH + 1) * TPS), 0, 1 << 19, dtype=jnp.int32)
    ranking = noise * 1024 + candidate[None, :]
    ranking = jnp.where(usable, ranking, (1 << 30) + candidate[None, :])
    ranking = jnp.where(candidate[None, :] == far_cand[:, None], -1, ranking)
    ranking = jnp.where(candidate[None, :] == own_cand[:, None], -2, ranking)
    picked = jnp.argsort(ranking, axis=1, stable=True)[:, :KT].astype(jnp.int32)
    chosen = (tile_slab[:, None] + picked // TPS - REACH) * TPS + picked % TPS
    return chosen.astype(jnp.int32)


def levels(own_key, shape, shards, smallest, top_value):
    def one(dim, shards_of):
        draws = jax.random.uniform(jax.random.fold_in(jax.random.fold_in(own_key, 6), dim), (shards_of,), jnp.float32, smallest / len(shards), top_value / len(shards))
        return jnp.repeat(jnp.exp(draws), shape[dim] // shards_of).reshape((-1,) + (1,) * (len(shape) - dim - 1))

    loudness = one(*shards[0])
    for cut in shards[1:]:
        loudness = loudness * one(*cut)
    return loudness


def gaussian(key, shape, deviation, bound, pieces=(), kind=jnp.bfloat16):
    loudness = levels(key, shape, pieces, -0.22, 0.18) if pieces else 1.0
    values = jax.random.normal(key, shape, jnp.float32) * deviation * loudness
    return jnp.minimum(jnp.maximum(values, -bound), bound).astype(kind)


def setup_inputs(seed: int = 0, part: int = 0) -> dict:
    seeds = jax.random.split(jax.random.key(seed), 6)
    part_keys = jax.random.split(jax.random.fold_in(seeds[5], part), 6)
    return {
        "query": draw_query(jax.random.fold_in(jax.random.fold_in(seeds[5], part), 71), part),
        "keys": draw_keys(jax.random.fold_in(jax.random.fold_in(seeds[5], part), 71), part),
        "values": gaussian(part_keys[2], (TOKENS, HEADS * HD), 1.0, 6.0, ((0, 16), (1, 8))),
        "out_weight": gaussian(seeds[3], (HEADS * HD, D), HD ** -0.5, 0.5, ((0, 8),)),
        "tile_lists": draw_tile_lists(jax.random.fold_in(jax.random.fold_in(seeds[5], part), 71), part),
    }


def reference(query, keys, values, out_weight, tile_lists):
    score_scale = 1.0 / math.sqrt(HD)
    query_tiles = query.reshape(NTILES, TILE, HEADS, HD)
    key_tiles = keys.reshape(NTILES, TILE, HEADS, HD)
    value_tiles = values.reshape(NTILES, TILE, HEADS, HD)

    def one_tile(block):
        query_tile, id_row = block
        key_rows = key_tiles[id_row].reshape(KT * TILE, HEADS, HD).astype(jnp.float32)
        value_rows = value_tiles[id_row].reshape(KT * TILE, HEADS, HD).astype(jnp.float32)
        scores = jnp.einsum('qhd,khd->hqk', query_tile.astype(jnp.float32), key_rows) * score_scale
        row_max = lax.optimization_barrier(jnp.max(scores, axis=-1, keepdims=True))
        exp_scores = jnp.exp(scores - row_max)
        row_total = lax.optimization_barrier(jnp.sum(exp_scores, axis=-1, keepdims=True))
        weights = lax.optimization_barrier(exp_scores.astype(jnp.bfloat16)).astype(jnp.float32)
        mixed_tile = jnp.einsum('hqk,khd->qhd', weights, value_rows) / jnp.transpose(row_total, (1, 0, 2))
        return mixed_tile.astype(jnp.bfloat16)
    attended = lax.map(one_tile, (query_tiles, tile_lists)).reshape(TOKENS, HEADS * HD)
    running_sum = jnp.zeros((TOKENS, D), jnp.float32)
    for group_index in range(HEADS * HD // HEAD_COLS):
        first_col = group_index * HEAD_COLS
        partial_sum = jnp.dot(attended[:, first_col:first_col + HEAD_COLS], out_weight[first_col:first_col + HEAD_COLS], preferred_element_type=jnp.float32)
        running_sum = running_sum + lax.optimization_barrier(partial_sum.astype(jnp.bfloat16)).astype(jnp.float32)
    return running_sum.astype(jnp.bfloat16)
```

```python
import functools
import math

import jax
import jax.numpy as jnp
from jax import lax
from jax.experimental import pallas as pl
from jax.experimental.pallas import tpu as pltpu
from jax.sharding import PartitionSpec as P

HD = 128
TILE = 384
CHUNK = 192
SCALE = math.log2(math.e) / math.sqrt(HD)
PLACE = ("frame", "head")


def attend_kernel(ids, q_ref, *refs):
    slabs, (o_ref, key_bank, value_bank, even, odd, sems) = refs[:5], refs[5:]
    tokens = q_ref.shape[0]
    listed = ids.shape[1]
    chunks = tokens // CHUNK
    copies = []
    for i, slab in enumerate(slabs):
        rows = pl.ds(i * tokens, tokens)
        copies.append(
            pltpu.make_async_copy(slab.at[:, 0:HD], key_bank.at[rows, :], sems.at[2 * i])
        )
        copies.append(
            pltpu.make_async_copy(
                slab.at[:, HD : 2 * HD], value_bank.at[rows, 0:HD], sems.at[2 * i + 1]
            )
        )
    for copy in copies:
        copy.start()
    value_bank[:, HD : 2 * HD] = jnp.ones((len(slabs) * tokens, HD), jnp.bfloat16)
    for copy in copies:
        copy.wait()

    def tile_rows(chunk, j):
        return pl.ds(pl.multiple_of(ids[chunk * CHUNK // TILE, j] * TILE, TILE), TILE)

    def chunk_rows(chunk):
        return pl.ds(pl.multiple_of(chunk * CHUNK, CHUNK), CHUNK)

    def score(chunk, store, j):
        tile_scores = lax.dot_general(
            q_ref[chunk_rows(chunk), :],
            key_bank[tile_rows(chunk, j), :],
            (((1,), (1,)), ((), ())),
            preferred_element_type=jnp.float32,
        )
        store[:, j * TILE : (j + 1) * TILE] = tile_scores
        return functools.reduce(
            jnp.maximum, [tile_scores[:, i : i + HD] for i in range(0, TILE, HD)]
        )

    def weigh(chunk, store, j, row_max):
        weights = jnp.exp2(store[:, j * TILE : (j + 1) * TILE] * SCALE - row_max)
        return jnp.dot(
            weights.astype(jnp.bfloat16),
            value_bank[tile_rows(chunk, j), :],
            preferred_element_type=jnp.float32,
        )

    def finish(chunk, total):
        o_ref[chunk_rows(chunk), :] = (total[:, 0:HD] / total[:, HD : 2 * HD]).astype(jnp.bfloat16)

    def row_limit(lane_max):
        return jnp.max(lane_max, axis=1, keepdims=True) * SCALE

    def both(chunk, now, later, row_max):
        lane_max, total = None, None
        for j in range(listed):
            found = score(chunk + 1, later, j)
            lane_max = found if lane_max is None else jnp.maximum(lane_max, found)
            term = weigh(chunk, now, j, row_max)
            total = term if total is None else total + term
        finish(chunk, total)
        return row_limit(lane_max)

    def pair(step, row_max):
        row_max = both(2 * step, even, odd, row_max)
        return both(2 * step + 1, odd, even, row_max)

    row_max = row_limit(
        functools.reduce(jnp.maximum, [score(0, even, j) for j in range(listed)])
    )
    row_max = lax.fori_loop(0, chunks // 2 - 1, pair, row_max)
    row_max = both(chunks - 2, even, odd, row_max)
    total = functools.reduce(
        jnp.add, [weigh(chunks - 1, odd, j, row_max) for j in range(listed)]
    )
    finish(chunks - 1, total)


def attend(ids, query, slabs):
    tokens = query.shape[0]
    listed = ids.shape[1]
    products = tokens * listed * TILE
    in_hbm = pl.BlockSpec(memory_space=pltpu.MemorySpace.HBM)
    in_vmem = pl.BlockSpec(memory_space=pltpu.MemorySpace.VMEM)
    return pl.pallas_call(
        attend_kernel,
        out_shape=jax.ShapeDtypeStruct((tokens, HD), jnp.bfloat16),
        in_specs=[pl.BlockSpec(memory_space=pltpu.MemorySpace.SMEM), in_vmem] + [in_hbm] * 5,
        out_specs=in_vmem,
        scratch_shapes=[
            pltpu.VMEM((5 * tokens, HD), jnp.bfloat16),
            pltpu.VMEM((5 * tokens, 2 * HD), jnp.bfloat16),
            pltpu.VMEM((CHUNK, listed * TILE), jnp.float32),
            pltpu.VMEM((CHUNK, listed * TILE), jnp.float32),
            pltpu.SemaphoreType.DMA((10,)),
        ],
        compiler_params=pltpu.CompilerParams(vmem_limit_bytes=40 * 1024 * 1024),
        cost_estimate=pl.CostEstimate(
            flops=8 * products * HD, bytes_accessed=20 * tokens * HD, transcendentals=products
        ),
    )(ids, query, *slabs)


def on_device(query, keys, values, out_weight, tile_lists):
    frames = lax.axis_size("frame")
    groups = lax.axis_size("head")
    heads_here = query.shape[1] // HD
    tiles_here = query.shape[0] // TILE
    frame = lax.axis_index("frame")
    head = lax.axis_index("head")

    def route(target):
        pairs = []
        for z in range(frames // 2):
            for a in range(2):
                for y in range(groups // 2):
                    for c in range(2):
                        z2, a2, c2 = target(z, a, c)
                        if 0 <= z2 < frames // 2:
                            source = (2 * z + a) * groups + 2 * y + c
                            pairs.append((source, (2 * z2 + a2) * groups + 2 * y + c2))
        return pairs

    turn = route(lambda z, a, c: (z, c, a))
    near = route(lambda z, a, c: (z - 1 if c == 0 else z + 1, a, c))
    far = route(lambda z, a, c: (z + 1 if c == 0 else z - 1, a, c))
    swap = route(lambda z, a, c: (z, a, 1 - c))

    def move(block, pairs):
        return lax.ppermute(block, PLACE, pairs)

    core = head % 2
    slab = frame // 2 * 2 + core
    lists = move(tile_lists, turn)
    offset = lists // tiles_here - slab
    place = jnp.where(
        core == 0,
        jnp.array([4, 3, 0, 1, 2], jnp.int32)[offset + 2],
        jnp.array([2, 1, 0, 3, 4], jnp.int32)[offset + 2],
    )
    ids = place * tiles_here + lists % tiles_here

    columns = [slice(h * HD, (h + 1) * HD) for h in range(heads_here)]
    mixed = None
    for cols in columns:
        own = move(jnp.concatenate([keys[:, cols], values[:, cols]], axis=1), turn)
        turned_query = move(query[:, cols], turn)
        shared = move(own, near)
        other = move(own, swap)
        crossed = move(shared, swap)
        edge = move(own, far)
        attended = attend(ids, turned_query, [own, other, shared, crossed, edge])
        attended = move(attended, turn)
        rows = lax.all_to_all(attended, "head", 0, 1, tiled=True)
        weight = lax.all_gather(out_weight[cols, :], "head", axis=0, tiled=True)
        term = jnp.dot(rows, weight, preferred_element_type=jnp.float32)
        mixed = term if mixed is None else mixed + term
    return mixed.astype(jnp.bfloat16)


def solution(mesh):
    return jax.shard_map(
        on_device,
        mesh=mesh,
        in_specs=(
            P(("video", "frame"), "head"),
            P(("video", "frame"), "head"),
            P(("video", "frame"), "head"),
            P("head", None),
            P(("video", "frame"), None),
        ),
        out_specs=P(("video", "frame", "head"), None),
        check_vma=False,
    )
```

```python
import functools
import math

import jax
import jax.numpy as jnp
from jax import lax
from jax.experimental import pallas as pl
from jax.experimental.pallas import tpu as pltpu
from jax.sharding import PartitionSpec as P

HD = 128
TILE = 384
CHUNK = 192
JOINED = 6
SCALE = math.log2(math.e) / math.sqrt(HD)
PROJ_FLOPS = 3_000_000_000
PLACE = ("frame", "head")
ATT_FLOPS = 10_000_000_000


def attend_kernel(first, ids, inner, query, own, other, *refs):
    inner_slabs, outer_slabs = refs[0:3], refs[3:6]
    o_ref, q_ref, key_bank, value_bank, even, odd, sems = refs[6:]
    tokens = o_ref.shape[0]
    heads = key_bank.shape[0]
    width = own.shape[1] // 2

    def transfer(kind, head, then):
        at = kind * width + (first + head) * HD

        def copy(i, ref):
            rows = pl.ds(i * tokens, tokens)
            bank = (key_bank.at[head, rows, :], value_bank.at[head, rows, 0:HD])[kind]
            moved = pltpu.make_async_copy(
                ref.at[:, at : at + HD], bank, sems.at[head, 2 * i + kind]
            )
            getattr(moved, then)()

        copy(0, own)
        copy(1, other)

        @pl.when(inner[0] == 1)
        def _():
            for i in range(3):
                copy(2 + i, inner_slabs[i])

        @pl.when(inner[0] == 0)
        def _():
            for i in range(3):
                copy(2 + i, outer_slabs[i])

    asked = pltpu.make_async_copy(
        query.at[pl.ds(0, tokens), first * HD : (first + heads) * HD], q_ref, sems.at[0, 10]
    )
    asked.start()
    for head in range(heads):
        transfer(0, head, "start")
        transfer(1, head, "start")
    for head in range(heads):
        value_bank[head, :, HD : 2 * HD] = jnp.ones((5 * tokens, HD), jnp.bfloat16)
    asked.wait()
    for head in range(heads):
        cols = slice(head * HD, (head + 1) * HD)
        attend_head(
            ids,
            q_ref.at[:, cols],
            key_bank.at[head],
            value_bank.at[head],
            o_ref.at[:, cols],
            even,
            odd,
            functools.partial(transfer, head=head, then="wait"),
        )


def attend_head(ids, q_ref, key_bank, value_bank, o_ref, even, odd, ready):
    listed = ids.shape[1]
    chunks = o_ref.shape[0] // CHUNK

    def tile_rows(chunk, j):
        return pl.ds(pl.multiple_of(ids[chunk * CHUNK // TILE, j] * TILE, TILE), TILE)

    def chunk_rows(chunk):
        return pl.ds(pl.multiple_of(chunk * CHUNK, CHUNK), CHUNK)

    def score(chunk, store, j):
        tile_scores = lax.dot_general(
            q_ref[chunk_rows(chunk), :],
            key_bank[tile_rows(chunk, j), :],
            (((1,), (1,)), ((), ())),
            preferred_element_type=jnp.float32,
        )
        store[:, j * TILE : (j + 1) * TILE] = tile_scores
        return functools.reduce(
            jnp.maximum, [tile_scores[:, i : i + HD] for i in range(0, TILE, HD)]
        )

    def weigh(chunk, store, j, row_max):
        weights = jnp.exp2(store[:, j * TILE : (j + JOINED) * TILE] * SCALE - row_max)
        tiles = [value_bank[tile_rows(chunk, j + i), :] for i in range(JOINED)]
        return jnp.dot(
            weights.astype(jnp.bfloat16),
            jnp.concatenate(tiles, axis=0),
            preferred_element_type=jnp.float32,
        )

    def finish(chunk, total):
        o_ref[chunk_rows(chunk), :] = (total[:, 0:HD] / total[:, HD : 2 * HD]).astype(jnp.bfloat16)

    def row_limit(lane_max):
        return jnp.max(lane_max, axis=1, keepdims=True) * SCALE

    def both(chunk, now, later, row_max):
        lane_max, total = None, None
        for j in range(listed):
            found = score(chunk + 1, later, j)
            lane_max = found if lane_max is None else jnp.maximum(lane_max, found)
            if (j + 1) % JOINED == 0:
                term = weigh(chunk, now, j + 1 - JOINED, row_max)
                total = term if total is None else total + term
        finish(chunk, total)
        return row_limit(lane_max)

    def pair(step, row_max):
        row_max = both(2 * step, even, odd, row_max)
        return both(2 * step + 1, odd, even, row_max)

    ready(0)
    row_max = row_limit(
        functools.reduce(jnp.maximum, [score(0, even, j) for j in range(listed)])
    )
    ready(1)
    row_max = lax.fori_loop(0, chunks // 2 - 1, pair, row_max)
    row_max = both(chunks - 2, even, odd, row_max)
    total = functools.reduce(
        jnp.add, [weigh(chunks - 1, odd, j, row_max) for j in range(0, listed, JOINED)]
    )
    finish(chunks - 1, total)


def attend(ids, inner, first, heads, arrays):
    tokens = arrays[1].shape[0]
    listed = ids.shape[1]
    anywhere = pl.BlockSpec(memory_space=pl.ANY)
    in_smem = pl.BlockSpec(memory_space=pltpu.MemorySpace.SMEM)
    return pl.pallas_call(
        functools.partial(attend_kernel, first),
        out_shape=jax.ShapeDtypeStruct((tokens, heads * HD), jnp.bfloat16),
        in_specs=[in_smem, in_smem] + [anywhere] * len(arrays),
        out_specs=pl.BlockSpec(memory_space=pltpu.MemorySpace.VMEM),
        scratch_shapes=[
            pltpu.VMEM((tokens, heads * HD), jnp.bfloat16),
            pltpu.VMEM((heads, 5 * tokens, HD), jnp.bfloat16),
            pltpu.VMEM((heads, 5 * tokens, 2 * HD), jnp.bfloat16),
            pltpu.VMEM((CHUNK, listed * TILE), jnp.float32),
            pltpu.VMEM((CHUNK, listed * TILE), jnp.float32),
            pltpu.SemaphoreType.DMA((heads, 11)),
        ],
        compiler_params=pltpu.CompilerParams(vmem_limit_bytes=56 * 1024 * 1024),
        cost_estimate=pl.CostEstimate(
            flops=heads * ATT_FLOPS, bytes_accessed=1024, transcendentals=0
        ),
        name="attend",
    )(ids, inner, *arrays)


def project_kernel(rows, weight, *refs):
    out, packed = refs[-2], refs[-1]
    groups, _, width = rows.shape

    @pl.when(pl.program_id(0) == 0)
    def _():
        for g in range(groups):
            packed[:, g * width : (g + 1) * width] = rows[g]

    total = jnp.dot(
        packed[...],
        weight[...].reshape(groups * width, weight.shape[-1]),
        preferred_element_type=jnp.float32,
    )
    if len(refs) > 2:
        total = total + refs[0][...]
    out[...] = total.astype(out.dtype)


def project(rows, weight, place, earlier):
    groups, tokens, width = rows.shape
    columns = weight.shape[-1]
    step = 1024
    part = pl.BlockSpec((tokens, step), lambda i: (0, i))
    return pl.pallas_call(
        project_kernel,
        out_shape=jax.ShapeDtypeStruct(
            (tokens, columns), jnp.float32 if earlier is None else jnp.bfloat16
        ),
        grid=(columns // step,),
        in_specs=[
            pl.BlockSpec((groups, tokens, width), lambda i: (0, 0, 0)),
            pl.BlockSpec((groups, width, step), lambda i: (0, place, i)),
        ]
        + ([] if earlier is None else [part]),
        out_specs=part,
        scratch_shapes=[pltpu.VMEM((tokens, groups * width), jnp.bfloat16)],
        compiler_params=pltpu.CompilerParams(vmem_limit_bytes=56 * 1024 * 1024),
        cost_estimate=pl.CostEstimate(flops=PROJ_FLOPS, bytes_accessed=1024, transcendentals=0),
        name="project",
    )(rows, weight, *([] if earlier is None else [earlier]))


def after(value, *earlier):
    return lax.optimization_barrier((value, *earlier))[0]


def on_device(query, keys, values, out_weight, tile_lists):
    frames = lax.axis_size("frame")
    groups = lax.axis_size("head")
    heads_here = query.shape[1] // HD
    tokens = query.shape[0]
    tiles_here = tokens // TILE
    frame = lax.axis_index("frame")
    head = lax.axis_index("head")

    def route(target, chosen=lambda a, c: True):
        pairs = []
        for z in range(frames // 2):
            for a in range(2):
                for y in range(groups // 2):
                    for c in range(2):
                        z2, a2, c2 = target(z, a, c)
                        if 0 <= z2 < frames // 2 and chosen(a, c):
                            source = (2 * z + a) * groups + 2 * y + c
                            pairs.append((source, (2 * z2 + a2) * groups + 2 * y + c2))
        return pairs

    def is_inner(a, c):
        return a == c

    def is_outer(a, c):
        return a != c

    def to_near(z, a, c):
        return z - 1 if c == 0 else z + 1, a, c

    def to_far(z, a, c):
        return z + 1 if c == 0 else z - 1, a, c

    def to_core(z, a, c):
        return z, a, 1 - c

    turn = route(lambda z, a, c: (z, c, a))
    swap = route(to_core)

    def move(block, pairs):
        return lax.ppermute(block, PLACE, pairs)

    weight = lax.all_gather(out_weight, "head", axis=0, tiled=True)
    weight = weight.reshape(groups, heads_here * HD, out_weight.shape[1])

    pair = jnp.concatenate([keys, values], axis=1)
    own = move(pair, turn)
    inner_near = move(pair, route(to_near, is_inner))
    inner_far = move(pair, route(to_far, is_inner))
    noted = jnp.pad(
        tile_lists.astype(jnp.bfloat16),
        ((0, 16 - tiles_here), (0, query.shape[1] - tile_lists.shape[1])),
    )
    asked = jnp.concatenate([query, noted], axis=0)
    ready = after(own, inner_near, inner_far)
    near = move(ready, route(to_near, is_outer))
    far = move(ready, route(to_far, is_outer))
    other = move(own, swap)
    asked = move(after(asked, other), turn)
    inner_crossed = move(inner_near, route(to_core, is_inner))
    crossed = move(after(near, asked), route(to_core, is_outer))

    core = head % 2
    slab = frame // 2 * 2 + core
    inner = (frame % 2 == core).astype(jnp.int32).reshape(1)
    lists = asked[tokens : tokens + tiles_here, 0 : tile_lists.shape[1]].astype(jnp.int32)
    offset = lists // tiles_here - slab
    side = jnp.where(core == 0, offset, -offset)
    place = jnp.where(side == -2, 4, jnp.where(side == -1, 3, jnp.where(side == 0, 0, side)))
    ids = place * tiles_here + lists % tiles_here

    arrays = [asked, own, other, inner_near, crossed, inner_far, near, inner_crossed, far]
    early = attend(ids, inner, 0, 2, arrays)
    late = attend(after(ids, early), inner, 2, 1, arrays)

    def deliver(attended, width):
        return lax.all_to_all(
            attended.reshape(groups, -1, width * HD), "head", 0, 0, tiled=True
        )

    rows_early = deliver(after(move(early, turn), late), 2)
    rows_late = deliver(move(late, turn), 1)
    first = project(rows_early, weight, 0, None)
    return project(rows_late, weight, 2, first)


def solution(mesh):
    return jax.shard_map(
        on_device,
        mesh=mesh,
        in_specs=(
            P(("video", "frame"), "head"),
            P(("video", "frame"), "head"),
            P(("video", "frame"), "head"),
            P("head", None),
            P(("video", "frame"), None),
        ),
        out_specs=P(("video", "frame", "head"), None),
        check_vma=False,
    )
```

```python
import functools
import math

import jax
import jax.numpy as jnp
from jax import lax
from jax.experimental import pallas as pl
from jax.experimental.pallas import tpu as pltpu
from jax.sharding import PartitionSpec as P

HD = 128
TILE = 384
CHUNK = 192
JOINED = 6
SCALE = math.log2(math.e) / math.sqrt(HD)
PROJ_FLOPS = 3_000_000_000
PLACE = ("frame", "head")
ATT_FLOPS = 10_000_000_000


def attend_kernel(first, ids, inner, query, own, other, *refs):
    inner_slabs, outer_slabs = refs[0:3], refs[3:6]
    o_ref, q_ref, key_bank, value_bank, even, odd, sems = refs[6:]
    tokens = o_ref.shape[0]
    heads = key_bank.shape[0]
    width = own.shape[1] // 2

    def transfer(kind, head, then):
        at = kind * width + (first + head) * HD

        def copy(i, ref):
            rows = pl.ds(i * tokens, tokens)
            bank = (key_bank.at[head, rows, :], value_bank.at[head, rows, 0:HD])[kind]
            moved = pltpu.make_async_copy(
                ref.at[:, at : at + HD], bank, sems.at[head, 2 * i + kind]
            )
            getattr(moved, then)()

        copy(0, own)
        copy(1, other)

        @pl.when(inner[0] == 1)
        def _():
            for i in range(3):
                copy(2 + i, inner_slabs[i])

        @pl.when(inner[0] == 0)
        def _():
            for i in range(3):
                copy(2 + i, outer_slabs[i])

    asked = pltpu.make_async_copy(
        query.at[pl.ds(0, tokens), first * HD : (first + heads) * HD], q_ref, sems.at[0, 10]
    )
    asked.start()
    for head in range(heads):
        transfer(0, head, "start")
        transfer(1, head, "start")
    for head in range(heads):
        value_bank[head, :, HD : 2 * HD] = jnp.ones((5 * tokens, HD), jnp.bfloat16)
    asked.wait()
    for head in range(heads):
        cols = slice(head * HD, (head + 1) * HD)
        attend_head(
            ids,
            q_ref.at[:, cols],
            key_bank.at[head],
            value_bank.at[head],
            o_ref.at[:, cols],
            even,
            odd,
            functools.partial(transfer, head=head, then="wait"),
        )


def attend_head(ids, q_ref, key_bank, value_bank, o_ref, even, odd, ready):
    listed = ids.shape[1]
    chunks = o_ref.shape[0] // CHUNK

    def tile_rows(chunk, j):
        return pl.ds(pl.multiple_of(ids[chunk * CHUNK // TILE, j] * TILE, TILE), TILE)

    def chunk_rows(chunk):
        return pl.ds(pl.multiple_of(chunk * CHUNK, CHUNK), CHUNK)

    def score(chunk, store, j):
        tile_scores = lax.dot_general(
            q_ref[chunk_rows(chunk), :],
            key_bank[tile_rows(chunk, j), :],
            (((1,), (1,)), ((), ())),
            preferred_element_type=jnp.float32,
        )
        store[:, j * TILE : (j + 1) * TILE] = tile_scores
        return functools.reduce(
            jnp.maximum, [tile_scores[:, i : i + HD] for i in range(0, TILE, HD)]
        )

    def weigh(chunk, store, j, row_max):
        weights = jnp.exp2(store[:, j * TILE : (j + JOINED) * TILE] * SCALE - row_max)
        tiles = [value_bank[tile_rows(chunk, j + i), :] for i in range(JOINED)]
        return jnp.dot(
            weights.astype(jnp.bfloat16),
            jnp.concatenate(tiles, axis=0),
            preferred_element_type=jnp.float32,
        )

    def finish(chunk, total):
        o_ref[chunk_rows(chunk), :] = (total[:, 0:HD] / total[:, HD : 2 * HD]).astype(jnp.bfloat16)

    def row_limit(lane_max):
        return jnp.max(lane_max, axis=1, keepdims=True) * SCALE

    def both(chunk, now, later, row_max):
        lane_max, total = None, None
        for j in range(listed):
            found = score(chunk + 1, later, j)
            lane_max = found if lane_max is None else jnp.maximum(lane_max, found)
            if (j + 1) % JOINED == 0:
                term = weigh(chunk, now, j + 1 - JOINED, row_max)
                total = term if total is None else total + term
        finish(chunk, total)
        return row_limit(lane_max)

    def pair(step, row_max):
        row_max = both(2 * step, even, odd, row_max)
        return both(2 * step + 1, odd, even, row_max)

    ready(0)
    row_max = row_limit(
        functools.reduce(jnp.maximum, [score(0, even, j) for j in range(listed)])
    )
    ready(1)
    row_max = lax.fori_loop(0, chunks // 2 - 1, pair, row_max)
    row_max = both(chunks - 2, even, odd, row_max)
    total = functools.reduce(
        jnp.add, [weigh(chunks - 1, odd, j, row_max) for j in range(0, listed, JOINED)]
    )
    finish(chunks - 1, total)


def attend(ids, inner, first, heads, arrays):
    tokens = arrays[1].shape[0]
    listed = ids.shape[1]
    anywhere = pl.BlockSpec(memory_space=pl.ANY)
    in_smem = pl.BlockSpec(memory_space=pltpu.MemorySpace.SMEM)
    return pl.pallas_call(
        functools.partial(attend_kernel, first),
        out_shape=jax.ShapeDtypeStruct((tokens, heads * HD), jnp.bfloat16),
        in_specs=[in_smem, in_smem] + [anywhere] * len(arrays),
        out_specs=pl.BlockSpec(memory_space=pltpu.MemorySpace.VMEM),
        scratch_shapes=[
            pltpu.VMEM((tokens, heads * HD), jnp.bfloat16),
            pltpu.VMEM((heads, 5 * tokens, HD), jnp.bfloat16),
            pltpu.VMEM((heads, 5 * tokens, 2 * HD), jnp.bfloat16),
            pltpu.VMEM((CHUNK, listed * TILE), jnp.float32),
            pltpu.VMEM((CHUNK, listed * TILE), jnp.float32),
            pltpu.SemaphoreType.DMA((heads, 11)),
        ],
        compiler_params=pltpu.CompilerParams(vmem_limit_bytes=56 * 1024 * 1024),
        cost_estimate=pl.CostEstimate(
            flops=heads * ATT_FLOPS, bytes_accessed=1024, transcendentals=0
        ),
        name="attend",
    )(ids, inner, *arrays)


def project_kernel(rows, weight, *refs):
    out, packed = refs[-2], refs[-1]
    groups, _, width = rows.shape

    @pl.when(pl.program_id(0) == 0)
    def _():
        for g in range(groups):
            packed[:, g * width : (g + 1) * width] = rows[g]

    total = jnp.dot(
        packed[...],
        weight[...].reshape(groups * width, weight.shape[-1]),
        preferred_element_type=jnp.float32,
    )
    if len(refs) > 2:
        total = total + refs[0][...]
    out[...] = total.astype(out.dtype)


def project(rows, weight, place, earlier):
    groups, tokens, width = rows.shape
    columns = weight.shape[-1]
    step = 1536
    part = pl.BlockSpec((tokens, step), lambda i: (0, i))
    return pl.pallas_call(
        project_kernel,
        out_shape=jax.ShapeDtypeStruct(
            (tokens, columns), jnp.float32 if earlier is None else jnp.bfloat16
        ),
        grid=(columns // step,),
        in_specs=[
            pl.BlockSpec((groups, tokens, width), lambda i: (0, 0, 0)),
            pl.BlockSpec((groups, width, step), lambda i: (0, place, i)),
        ]
        + ([] if earlier is None else [part]),
        out_specs=part,
        scratch_shapes=[pltpu.VMEM((tokens, groups * width), jnp.bfloat16)],
        compiler_params=pltpu.CompilerParams(vmem_limit_bytes=56 * 1024 * 1024),
        cost_estimate=pl.CostEstimate(flops=PROJ_FLOPS, bytes_accessed=1024, transcendentals=0),
        name="project",
    )(rows, weight, *([] if earlier is None else [earlier]))


def after(value, *earlier):
    return lax.optimization_barrier((value, *earlier))[0]


def on_device(query, keys, values, out_weight, tile_lists):
    frames = lax.axis_size("frame")
    groups = lax.axis_size("head")
    heads_here = query.shape[1] // HD
    tokens = query.shape[0]
    tiles_here = tokens // TILE
    frame = lax.axis_index("frame")
    head = lax.axis_index("head")

    def route(target, chosen=lambda a, c: True):
        pairs = []
        for z in range(frames // 2):
            for a in range(2):
                for y in range(groups // 2):
                    for c in range(2):
                        z2, a2, c2 = target(z, a, c)
                        if 0 <= z2 < frames // 2 and chosen(a, c):
                            source = (2 * z + a) * groups + 2 * y + c
                            pairs.append((source, (2 * z2 + a2) * groups + 2 * y + c2))
        return pairs

    def is_inner(a, c):
        return a == c

    def is_outer(a, c):
        return a != c

    def to_near(z, a, c):
        return z - 1 if c == 0 else z + 1, a, c

    def to_far(z, a, c):
        return z + 1 if c == 0 else z - 1, a, c

    def to_core(z, a, c):
        return z, a, 1 - c

    turn = route(lambda z, a, c: (z, c, a))
    swap = route(to_core)

    def move(block, pairs):
        return lax.ppermute(block, PLACE, pairs)

    weight = lax.all_gather(out_weight, "head", axis=0, tiled=True)
    weight = weight.reshape(groups, heads_here * HD, out_weight.shape[1])

    pair = jnp.concatenate([keys, values], axis=1)
    own = move(pair, turn)
    inner_near = move(pair, route(to_near, is_inner))
    inner_far = move(pair, route(to_far, is_inner))
    noted = jnp.pad(
        tile_lists.astype(jnp.bfloat16),
        ((0, 16 - tiles_here), (0, query.shape[1] - tile_lists.shape[1])),
    )
    asked = jnp.concatenate([query, noted], axis=0)
    ready = after(own, inner_near, inner_far)
    near = move(own, route(to_near, is_outer))
    far = move(ready, route(to_far, is_outer))
    other = move(own, swap)
    asked = move(after(asked, other), turn)
    inner_crossed = move(inner_near, route(to_core, is_inner))
    crossed = move(after(near, asked), route(to_core, is_outer))

    core = head % 2
    slab = frame // 2 * 2 + core
    inner = (frame % 2 == core).astype(jnp.int32).reshape(1)
    lists = asked[tokens : tokens + tiles_here, 0 : tile_lists.shape[1]].astype(jnp.int32)
    offset = lists // tiles_here - slab
    side = jnp.where(core == 0, offset, -offset)
    place = jnp.where(side == -2, 4, jnp.where(side == -1, 3, jnp.where(side == 0, 0, side)))
    ids = place * tiles_here + lists % tiles_here

    arrays = [asked, own, other, inner_near, crossed, inner_far, near, inner_crossed, far]
    early = attend(ids, inner, 0, 2, arrays)
    late = attend(after(ids, early), inner, 2, 1, arrays)

    def deliver(attended, width):
        return lax.all_to_all(
            attended.reshape(groups, -1, width * HD), "head", 0, 0, tiled=True
        )

    rows_early = deliver(after(move(early, turn), late), 2)
    rows_late = deliver(move(late, turn), 1)
    first = project(rows_early, weight, 0, None)
    return project(rows_late, weight, 2, first)


def solution(mesh):
    return jax.shard_map(
        on_device,
        mesh=mesh,
        in_specs=(
            P(("video", "frame"), "head"),
            P(("video", "frame"), "head"),
            P(("video", "frame"), "head"),
            P("head", None),
            P(("video", "frame"), None),
        ),
        out_specs=P(("video", "frame", "head"), None),
        check_vma=False,
    )
```
